256 devices in a mesh: dp: 64 (over y, z, x_lo), mp: 4 (over x_hi, core).
Axes of the slice: x: 4 (x_hi: 2, x_lo: 2; x = x_hi * 2 + x_lo), y: 4, z: 8, core: 2. Of those that a mesh axis runs over, the one named last changes fastest.
Arguments:
- activations: bfloat16 [32768, 6144], P('dp'), may hold values from -6 to 6
- gradients: bfloat16 [32768, 6144], P('dp'), may hold values from -2.5 to 2.5
- input_basis: bfloat16 [6144, 3072], P('dp', 'mp'), may hold values from -0.078125 to 0.078125
- output_basis: bfloat16 [6144, 3072], P('dp', 'mp'), may hold values from -0.078125 to 0.078125
Outputs:
- moments: float32 [3072, 3072], P('dp', 'mp')
The draws below stay inside these ranges and needn't reach their ends.
All inputs are finite; a program needn't handle non-finite values.
Results may differ from the reference program's by a relative error of at most 0.00098.
Values may be sent and summed in bfloat16 or wider, within the bound.
No kernel may reach another device: no remote copies, remote signals or barrier semaphores. Data moves between devices by JAX's collectives and lax.ppermute only.
A program may use at most 128 MiB of HBM per device.

```python
import jax
import jax.numpy as jnp
from jax import lax

D = 6144
KEEP = 3072
TOK_IMG = 256
IMAGES = 128


def spiked(values, rng, source, target, shards_of, factor):
    owner, partner = [(jnp.arange(values.shape[axis_at]) // (values.shape[axis_at] // shards_of)).reshape([-1 if axis == axis_at else 1 for axis in range(values.ndim)]) for axis_at in (source, target)]
    chosen = jax.random.permutation(rng, shards_of)[partner]
    strong = (owner == chosen) | (owner == (partner + shards_of // 2) % shards_of)
    return jnp.where(strong, factor * values, values)


def block_scale(stream_key, extent, shards, smallest, top_value):
    loudness = 1.0
    for axis_at, parts in shards:
        heights = jax.random.uniform(jax.random.fold_in(jax.random.fold_in(stream_key, 6), axis_at), (parts,), jnp.float32, smallest / len(shards), top_value / len(shards))
        loudness = loudness * jnp.repeat(jnp.exp(heights), extent[axis_at] // parts).reshape((-1,) + (1,) * (len(extent) - 1 - axis_at))
    return loudness


def normal_values(key, extent, deviation, limit, cuts=(), held_as=jnp.bfloat16):
    drawn = deviation * jax.random.normal(key, extent, jnp.float32)
    if cuts:
        drawn = drawn * block_scale(key, extent, cuts, -0.22, 0.18)
    return jnp.clip(drawn, -limit, limit).astype(held_as)


def noise_with(own_key, extent, scale, limit, pieces, heavy, kind=jnp.bfloat16):
    values = scale * jax.random.normal(own_key, extent, jnp.float32)
    if pieces:
        values = values * block_scale(own_key, extent, pieces, -0.22, 0.18)
    return jnp.clip(spiked(values, jax.random.fold_in(own_key, 3), *heavy), -limit, limit).astype(kind)


def setup_inputs(seed: int = 0) -> dict:
    splits = jax.random.split(jax.random.key(seed), 5)
    return {
        "activations": normal_values(splits[0], (IMAGES * TOK_IMG, D), 1.0, 6.0, ((0, 64),)),
        "gradients": noise_with(splits[1], (IMAGES * TOK_IMG, D), 0.0625, 2.5, ((0, 64),), (0, 1, 64, 4.0)),
        "input_basis": normal_values(splits[2], (D, KEEP), D ** -0.5, 0.078125, ((0, 64), (1, 4))),
        "output_basis": normal_values(splits[3], (D, KEEP), D ** -0.5, 0.078125, ((0, 64), (1, 4))),
    }


def reference(activations, gradients, input_basis, output_basis):
    rotated_inputs = jnp.dot(activations, input_basis, preferred_element_type=jnp.float32).astype(jnp.bfloat16)
    rotated_grads = jnp.dot(gradients, output_basis, preferred_element_type=jnp.float32).astype(jnp.bfloat16)
    width = input_basis.shape[1]
    stack_inputs = rotated_inputs.reshape(IMAGES, TOK_IMG, width)
    stack_grads = rotated_grads.reshape(IMAGES, TOK_IMG, width)

    def accumulate(total, pair):
        projected = jnp.dot(pair[0].T, pair[1], preferred_element_type=jnp.float32)
        return total + projected * projected, None

    total, unused = lax.scan(accumulate, jnp.zeros((width, width), jnp.float32), (stack_inputs, stack_grads))
    return total / IMAGES
```

```python
import jax
import jax.numpy as jnp
from jax import lax
from jax.sharding import PartitionSpec as P

TOK_IMG = 256
IMAGES = 128
NX, NY, NZ = 4, 4, 8
BOTH = ("dp", "mp")


def place(x, y, z, core):
    return ((y * NZ + z) * 2 + x % 2) * 4 + (x // 2) * 2 + core


def devices():
    for y in range(NY):
        for z in range(NZ):
            for x in range(NX):
                for core in range(2):
                    yield x, y, z, core


def route(move):
    pairs = [(at, move(*at)) for at in devices()]
    return [(place(*at), place(*to)) for at, to in pairs if to is not None]


def way(core):
    return 1 - 2 * core


RING_X = route(lambda x, y, z, c: ((x + way(c)) % NX, y, z, c))
RINGS_Y = [route(lambda x, y, z, c: (x, (y + s * way(c)) % NY, z, c)) for s in (1, -1)]
RINGS_Z = [route(lambda x, y, z, c: (x, y, (z + s * way(c)) % NZ, c)) for s in (1, -1)]
SHIFTS_Y = [route(lambda x, y, z, c: (x, (y + s) % NY, z, c)) for s in range(1, NY)]
SHIFTS_Z = [route(lambda x, y, z, c: (x, y, (z + s) % NZ, c)) for s in range(1, NZ)]
SWAP = route(lambda x, y, z, c: (x, y, z, 1 - c))
FORWARD = route(lambda x, y, z, c: (x, y, z, 1) if c == 0 else None)
PARTNER = route(lambda x, y, z, c: (x ^ 3 if c else x ^ 1, y, z, c))
DEAL_SAME = route(lambda x, y, z, c: (x // 2 * 2 + c, y, z, x % 2))
DEAL_OTHER = route(lambda x, y, z, c: (x // 2 * 2 + c, y, z, 1 - x % 2))


def home(x, y, z, core):
    panel = x ^ 1 if y // 2 else x
    columns = x ^ 3 if core else x
    return columns // 2 * 2 + y % 2, panel, z, columns % 2


HOME = route(home)


def send(value, pairs):
    return lax.ppermute(value, BOTH, pairs)


def ring_gather(block, at, step, size, rings, axis):
    gathered = jnp.zeros(block.shape[:axis] + (size,) + block.shape[axis:], block.dtype)
    gathered = lax.dynamic_update_index_in_dim(gathered, block, at, axis)
    moving = [block, block]
    for hop in range(1, size // 2 + 1):
        for side, sign in ((0, -step), (1, step)):
            if hop <= (size - side) // 2:
                moving[side] = send(moving[side], rings[side])
                gathered = lax.dynamic_update_index_in_dim(
                    gathered, moving[side], (at + sign * hop) % size, axis
                )
    return gathered


def shift_gather(block, at, size, shifts, axis):
    gathered = jnp.zeros(block.shape[:axis] + (size,) + block.shape[axis:], block.dtype)
    gathered = lax.dynamic_update_index_in_dim(gathered, block, at, axis)
    for offset in range(1, size):
        came = send(block, shifts[offset - 1])
        gathered = lax.dynamic_update_index_in_dim(gathered, came, (at - offset) % size, axis)
    return gathered


def ring_sum(blocks, at, step, size, rings):
    def part(away):
        return lax.dynamic_index_in_dim(blocks, (at + away) % size, 0, keepdims=False)

    total = part(0)
    for side, sign, hops in ((0, step, size // 2), (1, -step, size - 1 - size // 2)):
        running = part(sign * hops)
        for hop in range(hops - 1, -1, -1):
            running = send(running, rings[side])
            if hop:
                running = running + part(sign * hop)
        total = total + running
    return total


def shift_sum(blocks, at, size, shifts):
    def part(away):
        return lax.dynamic_index_in_dim(blocks, (at + away) % size, 0, keepdims=False)

    total = part(0)
    for offset in range(1, size):
        total = total + send(part(offset), shifts[offset - 1])
    return total


def dot(left, right):
    return jnp.dot(left, right, preferred_element_type=jnp.float32)


def on_device(activations, gradients, input_basis, output_basis):
    dp, mp = lax.axis_index("dp"), lax.axis_index("mp")
    core, x_lo, z, y = mp % 2, dp % 2, dp // 2 % NZ, dp // 2 // NZ
    step = 1 - 2 * core
    first = core == 0
    own = jnp.where(first, activations, gradients)
    other = send(own, RING_X)
    same = send(jnp.where(x_lo == 0, input_basis, output_basis), DEAL_SAME)
    cross = send(jnp.where(x_lo == 0, output_basis, input_basis), DEAL_OTHER)
    share = jnp.concatenate([jnp.where(first, same, cross), jnp.where(first, cross, same)], axis=0)
    width = share.shape[1]
    half = width // 2
    z_last = shift_gather(share[:, :half], y, NY, SHIFTS_Y, 0)
    z_last = ring_gather(z_last, z, step, NZ, RINGS_Z, 1).reshape(-1, half)
    y_last = ring_gather(share[:, half:], z, step, NZ, RINGS_Z, 0)
    y_last = ring_gather(y_last, y, step, NY, RINGS_Y, 0).reshape(-1, width - half)
    rotated_own, rotated_other = (
        jnp.concatenate([dot(rows, part).astype(jnp.bfloat16) for part in (z_last, y_last)], axis=1)
        for rows in (own, other)
    )
    squares = 0.0
    for mine, theirs in ((rotated_own, rotated_other), (rotated_other, rotated_own)):
        near = send(mine, SWAP)
        far = send(theirs, PARTNER)
        passed = send(far, FORWARD)
        inputs = jnp.concatenate(
            [jnp.where(first, mine, near), jnp.where(first, far, passed)], axis=1
        )
        grads = jnp.where(first, near, far)
        images = mine.shape[0] // TOK_IMG
        for image in range(images):
            rows = slice(image * TOK_IMG, (image + 1) * TOK_IMG)
            projected = lax.dot_general(
                inputs[rows],
                grads[rows],
                (((0,), (0,)), ((), ())),
                preferred_element_type=jnp.float32,
            )
            squares = squares + projected * projected
    depth = width // (2 * NZ)
    squares = squares.reshape(2, NZ, 2, depth, width)
    z_first = squares[..., :half].transpose(1, 0, 2, 3, 4).reshape(NZ, 4, depth, half)
    y_first = squares[..., half:].transpose(0, 2, 1, 3, 4).reshape(4, NZ, depth, half)
    left = shift_sum(ring_sum(z_first, z, step, NZ, RINGS_Z), y, NY, SHIFTS_Y)
    right = shift_sum(shift_sum(y_first, y, NY, SHIFTS_Y), z, NZ, SHIFTS_Z)
    total = jnp.concatenate([left, right], axis=1) * (1.0 / IMAGES)
    return send(total, HOME)


def solution(mesh):
    in_specs = (P("dp", None), P("dp", None), P("dp", "mp"), P("dp", "mp"))
    out_specs = P("dp", "mp")
    return jax.shard_map(
        on_device, mesh=mesh, in_specs=in_specs, out_specs=out_specs, check_vma=False
    )
```

```python
import jax
import jax.numpy as jnp
from jax import lax
from jax.experimental import pallas as pl
from jax.experimental.pallas import tpu as pltpu
from jax.sharding import PartitionSpec as P

TOK_IMG = 256
IMAGES = 128
NX, NY, NZ = 4, 4, 8
BOTH = ("dp", "mp")
LANES = 128
NOTE = 16
VMEM = 48 * 2**20


def place(x, y, z, core):
    return ((y * NZ + z) * 2 + x % 2) * 4 + (x // 2) * 2 + core


def devices():
    for y in range(NY):
        for z in range(NZ):
            for x in range(NX):
                for core in range(2):
                    yield x, y, z, core


def route(move):
    pairs = [(at, move(*at)) for at in devices()]
    return [(place(*at), place(*to)) for at, to in pairs if to is not None]


def way(core):
    return 1 - 2 * core


RING_X = route(lambda x, y, z, c: ((x + way(c)) % NX, y, z, c))
RINGS_Y = [route(lambda x, y, z, c: (x, (y + s * way(c)) % NY, z, c)) for s in (1, -1)]
RINGS_Z = [route(lambda x, y, z, c: (x, y, (z + s * way(c)) % NZ, c)) for s in (1, -1)]
SHIFTS_Y = [route(lambda x, y, z, c: (x, (y + s) % NY, z, c)) for s in range(1, NY)]
SHIFTS_Z = [route(lambda x, y, z, c: (x, y, (z + s) % NZ, c)) for s in range(1, NZ)]
LINES_Z = [
    [place(x, y, z, c) for z in range(NZ)]
    for x in range(NX)
    for y in range(NY)
    for c in range(2)
]
SWAP = route(lambda x, y, z, c: (x, y, z, 1 - c))
FORWARD = route(lambda x, y, z, c: (x, y, z, 1) if c == 0 else None)
PARTNER = route(lambda x, y, z, c: (x ^ 3 if c else x ^ 1, y, z, c))
DEAL_SAME = route(lambda x, y, z, c: (x // 2 * 2 + c, y, z, x % 2))
DEAL_OTHER = route(lambda x, y, z, c: (x // 2 * 2 + c, y, z, 1 - x % 2))


def home(x, y, z, core):
    panel = x ^ 1 if y // 2 else x
    columns = x ^ 3 if core else x
    return columns // 2 * 2 + y % 2, panel, z, columns % 2


HOME = route(home)


def send(value, pairs):
    return lax.ppermute(value, BOTH, pairs)


def hop(blocks, rings):
    return send(blocks[0], rings[0]), send(blocks[1], rings[1])


def ring_blocks(hops, at, step, size, axis):
    block = hops[0][0]
    gathered = jnp.zeros(block.shape[:axis] + (size,) + block.shape[axis:], block.dtype)
    for away, (up, down) in enumerate(hops):
        gathered = lax.dynamic_update_index_in_dim(gathered, up, (at - step * away) % size, axis)
        if 0 < away < size // 2:
            gathered = lax.dynamic_update_index_in_dim(
                gathered, down, (at + step * away) % size, axis
            )
    return gathered


def shift_gather(block, at, size, shifts, axis):
    gathered = jnp.zeros(block.shape[:axis] + (size,) + block.shape[axis:], block.dtype)
    gathered = lax.dynamic_update_index_in_dim(gathered, block, at, axis)
    for offset in range(1, size):
        came = send(block, shifts[offset - 1])
        gathered = lax.dynamic_update_index_in_dim(gathered, came, (at - offset) % size, axis)
    return gathered


def coded(sums):
    largest = jnp.max(jnp.max(sums, axis=0, keepdims=True), axis=1, keepdims=True)
    largest = jnp.where(largest > 1e-37, largest, 1.0).astype(jnp.bfloat16).astype(jnp.float32)
    ratio = sums * (1.0 / largest)
    square = ratio * ratio
    code = (square * square).astype(jnp.bfloat16)
    return code, jnp.broadcast_to(largest, (NOTE, sums.shape[1])).astype(jnp.bfloat16)


def decoded(block):
    code, note = block[:-NOTE].astype(jnp.float32), block[-NOTE:].astype(jnp.float32)
    return jnp.sqrt(jnp.sqrt(code)) * note[:1]


def moments_kernel(core_ref, *refs):
    mine, near, far, passed = refs[0:2], refs[2:4], refs[4:6], refs[6:8]
    z_out, y_out, tile_ref = refs[8:]
    which, half = pl.program_id(0), pl.program_id(1)
    tile = tile_ref.shape[0]
    columns = pl.ds(pl.multiple_of(half * tile, tile), tile)
    images = mine[0].shape[0] // TOK_IMG

    def add_up(inputs, grads):
        total = None
        for side in range(2):
            for image in range(images):
                rows = slice(image * TOK_IMG, (image + 1) * TOK_IMG)
                projected = lax.dot_general(
                    inputs[side][rows, columns],
                    grads[side][rows, :],
                    (((0,), (0,)), ((), ())),
                    preferred_element_type=jnp.float32,
                )
                total = projected * projected if total is None else total + projected * projected
        tile_ref[...] = total

    case = core_ref[0] * 2 + which
    for number, (inputs, grads) in enumerate(
        ((mine, near), (far, near), (near, far), (passed, far))
    ):
        pl.when(case == number)(lambda inputs=inputs, grads=grads: add_up(inputs, grads))
    code, note = coded(tile_ref[...])
    cut = z_out.shape[-1]
    places, band = z_out.shape[0], z_out.shape[2] - NOTE
    depth = band // 2
    for at in range(places):
        z_out[at, 0, :band, :] = code[at * band : (at + 1) * band, :cut]
        z_out[at, 0, band:, :] = note[:, :cut]
        for parity in range(2):
            start = at * band + parity * depth
            y_out[parity, 0, at * depth : (at + 1) * depth, :] = code[start : start + depth, cut:]
    for parity in range(2):
        y_out[parity, 0, places * depth :, :] = note[:, cut:]


def coded_moments(core, arrays, cut):
    rows, width = arrays[0].shape
    tile, places = width // 2, NZ // 2
    band = tile // places
    whole = pl.BlockSpec((rows, width), lambda i, j, c: (0, 0))
    return pl.pallas_call(
        moments_kernel,
        grid_spec=pltpu.PrefetchScalarGridSpec(
            num_scalar_prefetch=1,
            grid=(2, 2),
            in_specs=[whole] * len(arrays),
            out_specs=[
                pl.BlockSpec((places, 1, band + NOTE, cut), lambda i, j, c: (j, i, 0, 0)),
                pl.BlockSpec((2, 1, tile // 2 + NOTE, width - cut), lambda i, j, c: (i, j, 0, 0)),
            ],
            scratch_shapes=[pltpu.VMEM((tile, width), jnp.float32)],
        ),
        out_shape=[
            jax.ShapeDtypeStruct((NZ, 2, band + NOTE, cut), jnp.bfloat16),
            jax.ShapeDtypeStruct((NY, 2, tile // 2 + NOTE, width - cut), jnp.bfloat16),
        ],
        compiler_params=pltpu.CompilerParams(vmem_limit_bytes=VMEM),
        cost_estimate=pl.CostEstimate(
            flops=16 * rows * width * width, bytes_accessed=18 * rows * width, transcendentals=0
        ),
    )(core.reshape(1), *arrays)


def halfway_kernel(*refs):
    blocks, out = refs[:-1], refs[-1]
    came = [block.at[i] for block in blocks for i in range(block.shape[0])]
    bands = came[0].shape[0]
    sums = jnp.concatenate(
        [sum(decoded(block[band]) for block in came) for band in range(bands)], axis=0
    )
    code, note = coded(sums)
    depth = out.shape[1] - NOTE
    for at in range(out.shape[0]):
        out[at, :depth, :] = code[at * depth : (at + 1) * depth]
        out[at, depth:, :] = note


def halfway(blocks, size):
    bands, rows, columns = blocks[0].shape[1:]
    depth = bands * (rows - NOTE) // size
    return pl.pallas_call(
        halfway_kernel,
        out_shape=jax.ShapeDtypeStruct((size, depth + NOTE, columns), jnp.bfloat16),
        compiler_params=pltpu.CompilerParams(vmem_limit_bytes=VMEM),
        cost_estimate=pl.CostEstimate(flops=10**8, bytes_accessed=10**6, transcendentals=10**6),
    )(*blocks)


def final_kernel(*refs):
    left, right, out = refs[:-2], refs[-2], refs[-1]
    cut = left[0].shape[-1]
    came = [block.at[i] for block in left for i in range(block.shape[0])]
    out[:, :cut] = sum(decoded(block[...]) for block in came) * (1.0 / IMAGES)
    came = [right.at[i] for i in range(right.shape[0])]
    out[:, cut:] = sum(decoded(block[...]) for block in came) * (1.0 / IMAGES)


def final(left, right):
    size, rows, columns = right.shape
    shape = (rows - NOTE, left[0].shape[-1] + columns)
    return pl.pallas_call(
        final_kernel,
        out_shape=jax.ShapeDtypeStruct(shape, jnp.float32),
        compiler_params=pltpu.CompilerParams(vmem_limit_bytes=VMEM),
        cost_estimate=pl.CostEstimate(flops=10**7, bytes_accessed=10**6, transcendentals=10**6),
    )(*left, right)


def shift(to_send, at, size, shifts):
    offsets = sorted(range(size), key=lambda o: -min(o, size - o))
    picked = [lax.dynamic_slice_in_dim(to_send, (at + o) % size, 1, 0) for o in offsets]
    return [send(block, shifts[o - 1]) if o else block for o, block in zip(offsets, picked)]


def exchange(to_send, groups):
    return lax.all_to_all(to_send, BOTH, 0, 0, axis_index_groups=groups, tiled=True)


def rotate_kernel(rows_ref, left_ref, right_ref, out_ref, total_ref):
    basis = jnp.concatenate([left_ref[...], right_ref[...]], axis=1)
    product = jnp.dot(rows_ref[...], basis, preferred_element_type=jnp.float32)
    step = pl.program_id(0)

    @pl.when(step == 0)
    def _():
        total_ref[...] = product

    @pl.when(step > 0)
    def _():
        total_ref[...] += product

    @pl.when(step == pl.num_programs(0) - 1)
    def _():
        out_ref[...] = total_ref[...].astype(jnp.bfloat16)


def rotate(rows, left, right):
    count, long = rows.shape
    width = left.shape[1] + right.shape[1]
    depth = long // NY
    return pl.pallas_call(
        rotate_kernel,
        grid=(NY,),
        in_specs=[
            pl.BlockSpec((count, depth), lambda k: (0, k)),
            pl.BlockSpec((depth, left.shape[1]), lambda k: (k, 0)),
            pl.BlockSpec((depth, right.shape[1]), lambda k: (k, 0)),
        ],
        out_specs=pl.BlockSpec((count, width), lambda k: (0, 0)),
        out_shape=jax.ShapeDtypeStruct((count, width), jnp.bfloat16),
        scratch_shapes=[pltpu.VMEM((count, width), jnp.float32)],
        compiler_params=pltpu.CompilerParams(vmem_limit_bytes=VMEM),
        cost_estimate=pl.CostEstimate(
            flops=2 * count * long * width,
            bytes_accessed=2 * (count + width) * long,
            transcendentals=0,
        ),
    )(rows, left, right)


def on_device(activations, gradients, input_basis, output_basis):
    dp, mp = lax.axis_index("dp"), lax.axis_index("mp")
    core, x_lo, z, y = mp % 2, dp % 2, dp // 2 % NZ, dp // 2 // NZ
    step = 1 - 2 * core
    first = core == 0
    own = jnp.where(first, activations, gradients)
    same = send(jnp.where(x_lo == 0, input_basis, output_basis), DEAL_SAME)
    cross = send(jnp.where(x_lo == 0, output_basis, input_basis), DEAL_OTHER)
    share = jnp.concatenate([jnp.where(first, same, cross), jnp.where(first, cross, same)], axis=0)
    share, own = lax.optimization_barrier((share, own))
    other = send(own, RING_X)
    width = share.shape[1]
    half = width // 2
    z_last = shift_gather(share[:, :half], y, NY, SHIFTS_Y, 0)
    short = [(share[:, half:],) * 2]
    for _ in range(NZ // 2 - 1):
        short.append(hop(short[-1], RINGS_Z))
    short.append((send(short[-1][0], RINGS_Z[0]), None))
    z_last, short[-1] = lax.optimization_barrier((z_last, short[-1]))
    long_z = [(z_last,) * 2]
    for _ in range(2):
        long_z.append(hop(long_z[-1], RINGS_Z))
    long_y = [(ring_blocks(short, z, step, NZ, 0),) * 2]
    long_y.append(hop(long_y[-1], RINGS_Y))
    long_z.append(hop(long_z[-1], RINGS_Z))
    long_y.append((send(long_y[-1][0], RINGS_Y[0]), None))
    long_z.append((send(long_z[-1][0], RINGS_Z[0]), None))
    z_last = ring_blocks(long_z, z, step, NZ, 1).reshape(-1, half)
    y_last = ring_blocks(long_y, y, step, NY, 0).reshape(-1, width - half)
    rotated_own, rotated_other = (rotate(rows, z_last, y_last) for rows in (own, other))
    mine, theirs = (rotated_own, rotated_other), (rotated_other, rotated_own)
    near = [send(half, SWAP) for half in mine]
    far = [send(half, PARTNER) for half in theirs]
    passed = [send(half, FORWARD) for half in far]
    z_blocks, y_blocks = coded_moments(
        core, (*mine, *near, *far, *passed), width // 3 // LANES * LANES
    )
    came_z = exchange(z_blocks, LINES_Z)
    came_y = shift(y_blocks, y, NY, SHIFTS_Y)
    came_z, came_y = lax.optimization_barrier((came_z, came_y))
    left = shift(halfway([came_z], NY), y, NY, SHIFTS_Y)
    right = halfway(came_y, NZ)
    left, right = lax.optimization_barrier((left, right))
    total = final(left, exchange(right, LINES_Z))
    return send(total, HOME)


def solution(mesh):
    in_specs = (P("dp", None), P("dp", None), P("dp", "mp"), P("dp", "mp"))
    out_specs = P("dp", "mp")
    return jax.shard_map(
        on_device, mesh=mesh, in_specs=in_specs, out_specs=out_specs, check_vma=False
    )
```

```python
import jax
import jax.numpy as jnp
from jax import lax
from jax.experimental import pallas as pl
from jax.experimental.pallas import tpu as pltpu
from jax.sharding import PartitionSpec as P

TOK_IMG = 256
IMAGES = 128
NX, NY, NZ = 4, 4, 8
BOTH = ("dp", "mp")
LANES = 128
NOTE = 16
VMEM = 48 * 2**20


def place(x, y, z, core):
    return ((y * NZ + z) * 2 + x % 2) * 4 + (x // 2) * 2 + core


def devices():
    for y in range(NY):
        for z in range(NZ):
            for x in range(NX):
                for core in range(2):
                    yield x, y, z, core


def route(move):
    pairs = [(at, move(*at)) for at in devices()]
    return [(place(*at), place(*to)) for at, to in pairs if to is not None]


def way(core):
    return 1 - 2 * core


RING_X = route(lambda x, y, z, c: ((x + way(c)) % NX, y, z, c))
RINGS_Y = [route(lambda x, y, z, c: (x, (y + s * way(c)) % NY, z, c)) for s in (1, -1)]
RINGS_Z = [route(lambda x, y, z, c: (x, y, (z + s * way(c)) % NZ, c)) for s in (1, -1)]
SHIFTS_Y = [route(lambda x, y, z, c: (x, (y + s) % NY, z, c)) for s in range(1, NY)]
SHIFTS_Z = [route(lambda x, y, z, c: (x, y, (z + s) % NZ, c)) for s in range(1, NZ)]
LINES_Z = [
    [place(x, y, z, c) for z in range(NZ)]
    for x in range(NX)
    for y in range(NY)
    for c in range(2)
]
SWAP = route(lambda x, y, z, c: (x, y, z, 1 - c))
FORWARD = route(lambda x, y, z, c: (x, y, z, 1) if c == 0 else None)
PARTNER = route(lambda x, y, z, c: (x ^ 3 if c else x ^ 1, y, z, c))
DEAL_SAME = route(lambda x, y, z, c: (x // 2 * 2 + c, y, z, x % 2))
DEAL_OTHER = route(lambda x, y, z, c: (x // 2 * 2 + c, y, z, 1 - x % 2))


def home(x, y, z, core):
    panel = x ^ 1 if y // 2 else x
    columns = x ^ 3 if core else x
    return columns // 2 * 2 + y % 2, panel, z, columns % 2


HOME = route(home)


def send(value, pairs):
    return lax.ppermute(value, BOTH, pairs)


def hop(blocks, rings):
    return send(blocks[0], rings[0]), send(blocks[1], rings[1])


def ring_blocks(hops, at, step, size, axis):
    block = hops[0][0]
    gathered = jnp.zeros(block.shape[:axis] + (size,) + block.shape[axis:], block.dtype)
    for away, (up, down) in enumerate(hops):
        gathered = lax.dynamic_update_index_in_dim(gathered, up, (at - step * away) % size, axis)
        if 0 < away < size // 2:
            gathered = lax.dynamic_update_index_in_dim(
                gathered, down, (at + step * away) % size, axis
            )
    return gathered


def shift_gather(block, at, size, shifts, axis):
    gathered = jnp.zeros(block.shape[:axis] + (size,) + block.shape[axis:], block.dtype)
    gathered = lax.dynamic_update_index_in_dim(gathered, block, at, axis)
    for offset in range(1, size):
        came = send(block, shifts[offset - 1])
        gathered = lax.dynamic_update_index_in_dim(gathered, came, (at - offset) % size, axis)
    return gathered


def coded(sums):
    largest = jnp.max(jnp.max(sums, axis=0, keepdims=True), axis=1, keepdims=True)
    largest = jnp.where(largest > 1e-37, largest, 1.0).astype(jnp.bfloat16).astype(jnp.float32)
    ratio = sums * (1.0 / largest)
    square = ratio * ratio
    code = (square * square).astype(jnp.bfloat16)
    return code, jnp.broadcast_to(largest, (NOTE, sums.shape[1])).astype(jnp.bfloat16)


def decoded(block):
    code, note = block[:-NOTE].astype(jnp.float32), block[-NOTE:].astype(jnp.float32)
    return jnp.sqrt(jnp.sqrt(code)) * note[:1]


def moments_kernel(core_ref, *refs):
    mine, near, far, passed = refs[0:2], refs[2:4], refs[4:6], refs[6:8]
    z_out, y_out, tile_ref = refs[8:]
    which, half = pl.program_id(0), pl.program_id(1)
    tile = tile_ref.shape[0]
    columns = pl.ds(pl.multiple_of(half * tile, tile), tile)
    images = mine[0].shape[0] // TOK_IMG

    def add_up(inputs, grads):
        total = None
        for side in range(2):
            for image in range(images):
                rows = slice(image * TOK_IMG, (image + 1) * TOK_IMG)
                projected = lax.dot_general(
                    inputs[side][rows, columns],
                    grads[side][rows, :],
                    (((0,), (0,)), ((), ())),
                    preferred_element_type=jnp.float32,
                )
                total = projected * projected if total is None else total + projected * projected
        tile_ref[...] = total

    case = core_ref[0] * 2 + which
    for number, (inputs, grads) in enumerate(
        ((mine, near), (far, near), (near, far), (passed, far))
    ):
        pl.when(case == number)(lambda inputs=inputs, grads=grads: add_up(inputs, grads))
    code, note = coded(tile_ref[...])
    cut = z_out.shape[-1]
    places, band = z_out.shape[0], z_out.shape[2] - NOTE
    depth = band // 2
    for at in range(places):
        z_out[at, 0, :band, :] = code[at * band : (at + 1) * band, :cut]
        z_out[at, 0, band:, :] = note[:, :cut]
        for parity in range(2):
            start = at * band + parity * depth
            y_out[parity, 0, at * depth : (at + 1) * depth, :] = code[start : start + depth, cut:]
    for parity in range(2):
        y_out[parity, 0, places * depth :, :] = note[:, cut:]


def coded_moments(core, arrays, cut):
    rows, width = arrays[0].shape
    tile, places = width // 2, NZ // 2
    band = tile // places
    whole = pl.BlockSpec((rows, width), lambda i, j, c: (0, 0))
    return pl.pallas_call(
        moments_kernel,
        grid_spec=pltpu.PrefetchScalarGridSpec(
            num_scalar_prefetch=1,
            grid=(2, 2),
            in_specs=[whole] * len(arrays),
            out_specs=[
                pl.BlockSpec((places, 1, band + NOTE, cut), lambda i, j, c: (j, i, 0, 0)),
                pl.BlockSpec((2, 1, tile // 2 + NOTE, width - cut), lambda i, j, c: (i, j, 0, 0)),
            ],
            scratch_shapes=[pltpu.VMEM((tile, width), jnp.float32)],
        ),
        out_shape=[
            jax.ShapeDtypeStruct((NZ, 2, band + NOTE, cut), jnp.bfloat16),
            jax.ShapeDtypeStruct((NY, 2, tile // 2 + NOTE, width - cut), jnp.bfloat16),
        ],
        compiler_params=pltpu.CompilerParams(vmem_limit_bytes=VMEM),
        cost_estimate=pl.CostEstimate(
            flops=16 * rows * width * width, bytes_accessed=18 * rows * width, transcendentals=0
        ),
    )(core.reshape(1), *arrays)


def halfway_kernel(*refs):
    blocks, out = refs[:-1], refs[-1]
    came = [block.at[i] for block in blocks for i in range(block.shape[0])]
    bands = came[0].shape[0]
    sums = jnp.concatenate(
        [sum(decoded(block[band]) for block in came) for band in range(bands)], axis=0
    )
    code, note = coded(sums)
    depth = out.shape[1] - NOTE
    for at in range(out.shape[0]):
        out[at, :depth, :] = code[at * depth : (at + 1) * depth]
        out[at, depth:, :] = note


def halfway(blocks, size):
    bands, rows, columns = blocks[0].shape[1:]
    depth = bands * (rows - NOTE) // size
    return pl.pallas_call(
        halfway_kernel,
        out_shape=jax.ShapeDtypeStruct((size, depth + NOTE, columns), jnp.bfloat16),
        compiler_params=pltpu.CompilerParams(vmem_limit_bytes=VMEM),
        cost_estimate=pl.CostEstimate(flops=10**8, bytes_accessed=10**6, transcendentals=10**6),
    )(*blocks)


def final_kernel(*refs):
    left, right, out = refs[:-2], refs[-2], refs[-1]
    cut = left[0].shape[-1]
    came = [block.at[i] for block in left for i in range(block.shape[0])]
    out[:, :cut] = sum(decoded(block[...]) for block in came) * (1.0 / IMAGES)
    came = [right.at[i] for i in range(right.shape[0])]
    out[:, cut:] = sum(decoded(block[...]) for block in came) * (1.0 / IMAGES)


def final(left, right):
    size, rows, columns = right.shape
    shape = (rows - NOTE, left[0].shape[-1] + columns)
    return pl.pallas_call(
        final_kernel,
        out_shape=jax.ShapeDtypeStruct(shape, jnp.float32),
        compiler_params=pltpu.CompilerParams(vmem_limit_bytes=VMEM),
        cost_estimate=pl.CostEstimate(flops=10**7, bytes_accessed=10**6, transcendentals=10**6),
    )(*left, right)


def shift(to_send, at, size, shifts):
    offsets = sorted(range(size), key=lambda o: -min(o, size - o))
    picked = [lax.dynamic_slice_in_dim(to_send, (at + o) % size, 1, 0) for o in offsets]
    return [send(block, shifts[o - 1]) if o else block for o, block in zip(offsets, picked)]


def exchange(to_send, groups):
    return lax.all_to_all(to_send, BOTH, 0, 0, axis_index_groups=groups, tiled=True)


def rotate_kernel(rows_ref, left_ref, right_ref, out_ref, total_ref):
    basis = jnp.concatenate([left_ref[...], right_ref[...]], axis=1)
    product = jnp.dot(rows_ref[...], basis, preferred_element_type=jnp.float32)
    step = pl.program_id(0)

    @pl.when(step == 0)
    def _():
        total_ref[...] = product

    @pl.when(step > 0)
    def _():
        total_ref[...] += product

    @pl.when(step == pl.num_programs(0) - 1)
    def _():
        out_ref[...] = total_ref[...].astype(jnp.bfloat16)


def rotate(rows, left, right):
    count, long = rows.shape
    width = left.shape[1] + right.shape[1]
    depth = long // NY
    return pl.pallas_call(
        rotate_kernel,
        grid=(NY,),
        in_specs=[
            pl.BlockSpec((count, depth), lambda k: (0, k)),
            pl.BlockSpec((depth, left.shape[1]), lambda k: (k, 0)),
            pl.BlockSpec((depth, right.shape[1]), lambda k: (k, 0)),
        ],
        out_specs=pl.BlockSpec((count, width), lambda k: (0, 0)),
        out_shape=jax.ShapeDtypeStruct((count, width), jnp.bfloat16),
        scratch_shapes=[pltpu.VMEM((count, width), jnp.float32)],
        compiler_params=pltpu.CompilerParams(vmem_limit_bytes=VMEM),
        cost_estimate=pl.CostEstimate(
            flops=2 * count * long * width,
            bytes_accessed=2 * (count + width) * long,
            transcendentals=0,
        ),
    )(rows, left, right)


def on_device(activations, gradients, input_basis, output_basis):
    dp, mp = lax.axis_index("dp"), lax.axis_index("mp")
    core, x_lo, z, y = mp % 2, dp % 2, dp // 2 % NZ, dp // 2 // NZ
    step = 1 - 2 * core
    first = core == 0
    own = jnp.where(first, activations, gradients)
    same = send(jnp.where(x_lo == 0, input_basis, output_basis), DEAL_SAME)
    cross = send(jnp.where(x_lo == 0, output_basis, input_basis), DEAL_OTHER)
    share = jnp.concatenate([jnp.where(first, same, cross), jnp.where(first, cross, same)], axis=0)
    share, own = lax.optimization_barrier((share, own))
    other = send(own, RING_X)
    width = share.shape[1]
    half = width // 2
    short = [(share[:, half:],) * 2]
    short.append(hop(short[-1], RINGS_Z))
    left, short[-1] = lax.optimization_barrier((share[:, :half], short[-1]))
    for _ in range(NZ // 2 - 2):
        short.append(hop(short[-1], RINGS_Z))
    short.append((send(short[-1][0], RINGS_Z[0]), None))
    z_last = shift_gather(left, y, NY, SHIFTS_Y, 0)
    z_last, short[-1] = lax.optimization_barrier((z_last, short[-1]))
    long_z = [(z_last,) * 2]
    for _ in range(2):
        long_z.append(hop(long_z[-1], RINGS_Z))
    long_y = [(ring_blocks(short, z, step, NZ, 0),) * 2]
    long_y.append(hop(long_y[-1], RINGS_Y))
    long_z.append(hop(long_z[-1], RINGS_Z))
    long_y.append((send(long_y[-1][0], RINGS_Y[0]), None))
    long_z.append((send(long_z[-1][0], RINGS_Z[0]), None))
    z_last = ring_blocks(long_z, z, step, NZ, 1).reshape(-1, half)
    y_last = ring_blocks(long_y, y, step, NY, 0).reshape(-1, width - half)
    rotated_own, rotated_other = (rotate(rows, z_last, y_last) for rows in (own, other))
    mine, theirs = (rotated_own, rotated_other), (rotated_other, rotated_own)
    near = [send(half, SWAP) for half in mine]
    far = [send(half, PARTNER) for half in theirs]
    passed = [send(half, FORWARD) for half in far]
    z_blocks, y_blocks = coded_moments(
        core, (*mine, *near, *far, *passed), width // 3 // LANES * LANES
    )
    came_z = exchange(z_blocks, LINES_Z)
    came_y = shift(y_blocks, y, NY, SHIFTS_Y)
    left = shift(halfway([came_z], NY), y, NY, SHIFTS_Y)
    right = halfway(came_y, NZ)
    left, right = lax.optimization_barrier((left, right))
    total = final(left, exchange(right, LINES_Z))
    return send(total, HOME)


def solution(mesh):
    in_specs = (P("dp", None), P("dp", None), P("dp", "mp"), P("dp", "mp"))
    out_specs = P("dp", "mp")
    return jax.shard_map(
        on_device, mesh=mesh, in_specs=in_specs, out_specs=out_specs, check_vma=False
    )
```

```python
import jax
import jax.numpy as jnp
from jax import lax
from jax.experimental import pallas as pl
from jax.experimental.pallas import tpu as pltpu
from jax.sharding import PartitionSpec as P

TOK_IMG = 256
IMAGES = 128
NX, NY, NZ = 4, 4, 8
BOTH = ("dp", "mp")
LANES = 128
NOTE = 16
VMEM = 48 * 2**20


def place(x, y, z, core):
    return ((y * NZ + z) * 2 + x % 2) * 4 + (x // 2) * 2 + core


def devices():
    for y in range(NY):
        for z in range(NZ):
            for x in range(NX):
                for core in range(2):
                    yield x, y, z, core


def route(move):
    pairs = [(at, move(*at)) for at in devices()]
    return [(place(*at), place(*to)) for at, to in pairs if to is not None]


def way(core):
    return 1 - 2 * core


RING_X = route(lambda x, y, z, c: ((x + way(c)) % NX, y, z, c))
RINGS_Y = [route(lambda x, y, z, c: (x, (y + s * way(c)) % NY, z, c)) for s in (1, -1)]
RINGS_Z = [route(lambda x, y, z, c: (x, y, (z + s * way(c)) % NZ, c)) for s in (1, -1)]
SHIFTS_Y = [route(lambda x, y, z, c: (x, (y + s) % NY, z, c)) for s in range(1, NY)]
SHIFTS_Z = [route(lambda x, y, z, c: (x, y, (z + s) % NZ, c)) for s in range(1, NZ)]
LINES_Z = [
    [place(x, y, z, c) for z in range(NZ)]
    for x in range(NX)
    for y in range(NY)
    for c in range(2)
]
SWAP = route(lambda x, y, z, c: (x, y, z, 1 - c))
FORWARD = route(lambda x, y, z, c: (x, y, z, 1) if c == 0 else None)
PARTNER = route(lambda x, y, z, c: (x ^ 3 if c else x ^ 1, y, z, c))
DEAL_SAME = route(lambda x, y, z, c: (x // 2 * 2 + c, y, z, x % 2))
DEAL_OTHER = route(lambda x, y, z, c: (x // 2 * 2 + c, y, z, 1 - x % 2))


def home(x, y, z, core):
    panel = x ^ 1 if y // 2 else x
    columns = x ^ 3 if core else x
    return columns // 2 * 2 + y % 2, panel, z, columns % 2


HOME = route(home)


def send(value, pairs):
    return lax.ppermute(value, BOTH, pairs)


def hop(blocks, rings):
    return send(blocks[0], rings[0]), send(blocks[1], rings[1])


def ring_blocks(hops, at, step, size, axis):
    block = hops[0][0]
    gathered = jnp.zeros(block.shape[:axis] + (size,) + block.shape[axis:], block.dtype)
    for away, (up, down) in enumerate(hops):
        gathered = lax.dynamic_update_index_in_dim(gathered, up, (at - step * away) % size, axis)
        if 0 < away < size // 2:
            gathered = lax.dynamic_update_index_in_dim(
                gathered, down, (at + step * away) % size, axis
            )
    return gathered


def shift_gather(block, at, size, shifts, axis):
    gathered = jnp.zeros(block.shape[:axis] + (size,) + block.shape[axis:], block.dtype)
    gathered = lax.dynamic_update_index_in_dim(gathered, block, at, axis)
    for offset in range(1, size):
        came = send(block, shifts[offset - 1])
        gathered = lax.dynamic_update_index_in_dim(gathered, came, (at - offset) % size, axis)
    return gathered


def coded(sums):
    largest = jnp.max(jnp.max(sums, axis=0, keepdims=True), axis=1, keepdims=True)
    largest = jnp.where(largest > 1e-37, largest, 1.0).astype(jnp.bfloat16).astype(jnp.float32)
    ratio = sums * (1.0 / largest)
    square = ratio * ratio
    code = (square * square).astype(jnp.bfloat16)
    return code, jnp.broadcast_to(largest, (NOTE, sums.shape[1])).astype(jnp.bfloat16)


def decoded(block):
    code, note = block[:-NOTE].astype(jnp.float32), block[-NOTE:].astype(jnp.float32)
    return jnp.sqrt(jnp.sqrt(code)) * note[:1]


def moments_kernel(core_ref, *refs):
    mine, near, far, passed = refs[0:2], refs[2:4], refs[4:6], refs[6:8]
    z_out, y_out, tile_ref = refs[8:]
    which, half = pl.program_id(0), pl.program_id(1)
    tile = tile_ref.shape[0]
    columns = pl.ds(pl.multiple_of(half * tile, tile), tile)
    images = mine[0].shape[0] // TOK_IMG

    def add_up(inputs, grads):
        total = None
        for side in range(2):
            for image in range(images):
                rows = slice(image * TOK_IMG, (image + 1) * TOK_IMG)
                projected = lax.dot_general(
                    inputs[side][rows, columns],
                    grads[side][rows, :],
                    (((0,), (0,)), ((), ())),
                    preferred_element_type=jnp.float32,
                )
                total = projected * projected if total is None else total + projected * projected
        tile_ref[...] = total

    case = core_ref[0] * 2 + which
    for number, (inputs, grads) in enumerate(
        ((mine, near), (far, near), (near, far), (passed, far))
    ):
        pl.when(case == number)(lambda inputs=inputs, grads=grads: add_up(inputs, grads))
    code, note = coded(tile_ref[...])
    cut = z_out.shape[-1]
    places, band = z_out.shape[0], z_out.shape[2] - NOTE
    depth = band // 2
    for at in range(places):
        z_out[at, 0, :band, :] = code[at * band : (at + 1) * band, :cut]
        z_out[at, 0, band:, :] = note[:, :cut]
        for parity in range(2):
            start = at * band + parity * depth
            y_out[parity, 0, at * depth : (at + 1) * depth, :] = code[start : start + depth, cut:]
    for parity in range(2):
        y_out[parity, 0, places * depth :, :] = note[:, cut:]


def coded_moments(core, arrays, cut):
    rows, width = arrays[0].shape
    tile, places = width // 2, NZ // 2
    band = tile // places
    whole = pl.BlockSpec((rows, width), lambda i, j, c: (0, 0))
    return pl.pallas_call(
        moments_kernel,
        grid_spec=pltpu.PrefetchScalarGridSpec(
            num_scalar_prefetch=1,
            grid=(2, 2),
            in_specs=[whole] * len(arrays),
            out_specs=[
                pl.BlockSpec((places, 1, band + NOTE, cut), lambda i, j, c: (j, i, 0, 0)),
                pl.BlockSpec((2, 1, tile // 2 + NOTE, width - cut), lambda i, j, c: (i, j, 0, 0)),
            ],
            scratch_shapes=[pltpu.VMEM((tile, width), jnp.float32)],
        ),
        out_shape=[
            jax.ShapeDtypeStruct((NZ, 2, band + NOTE, cut), jnp.bfloat16),
            jax.ShapeDtypeStruct((NY, 2, tile // 2 + NOTE, width - cut), jnp.bfloat16),
        ],
        compiler_params=pltpu.CompilerParams(vmem_limit_bytes=VMEM),
        cost_estimate=pl.CostEstimate(
            flops=16 * rows * width * width, bytes_accessed=18 * rows * width, transcendentals=0
        ),
    )(core.reshape(1), *arrays)


def halfway_kernel(*refs):
    blocks, out = refs[:-1], refs[-1]
    came = [block.at[i] for block in blocks for i in range(block.shape[0])]
    bands = came[0].shape[0]
    sums = jnp.concatenate(
        [sum(decoded(block[band]) for block in came) for band in range(bands)], axis=0
    )
    code, note = coded(sums)
    depth = out.shape[1] - NOTE
    for at in range(out.shape[0]):
        out[at, :depth, :] = code[at * depth : (at + 1) * depth]
        out[at, depth:, :] = note


def halfway(blocks, size):
    bands, rows, columns = blocks[0].shape[1:]
    depth = bands * (rows - NOTE) // size
    return pl.pallas_call(
        halfway_kernel,
        out_shape=jax.ShapeDtypeStruct((size, depth + NOTE, columns), jnp.bfloat16),
        compiler_params=pltpu.CompilerParams(vmem_limit_bytes=VMEM),
        cost_estimate=pl.CostEstimate(flops=10**8, bytes_accessed=10**6, transcendentals=10**6),
    )(*blocks)


def final_kernel(*refs):
    left, right, out = refs[:-2], refs[-2], refs[-1]
    cut = left[0].shape[-1]
    came = [block.at[i] for block in left for i in range(block.shape[0])]
    out[:, :cut] = sum(decoded(block[...]) for block in came) * (1.0 / IMAGES)
    came = [right.at[i] for i in range(right.shape[0])]
    out[:, cut:] = sum(decoded(block[...]) for block in came) * (1.0 / IMAGES)


def final(left, right):
    size, rows, columns = right.shape
    shape = (rows - NOTE, left[0].shape[-1] + columns)
    return pl.pallas_call(
        final_kernel,
        out_shape=jax.ShapeDtypeStruct(shape, jnp.float32),
        compiler_params=pltpu.CompilerParams(vmem_limit_bytes=VMEM),
        cost_estimate=pl.CostEstimate(flops=10**7, bytes_accessed=10**6, transcendentals=10**6),
    )(*left, right)


def shift(to_send, at, size, shifts):
    offsets = sorted(range(size), key=lambda o: -min(o, size - o))
    picked = [lax.dynamic_slice_in_dim(to_send, (at + o) % size, 1, 0) for o in offsets]
    return [send(block, shifts[o - 1]) if o else block for o, block in zip(offsets, picked)]


def exchange(to_send, groups):
    return lax.all_to_all(to_send, BOTH, 0, 0, axis_index_groups=groups, tiled=True)


def rotate_kernel(rows_ref, left_ref, right_ref, out_ref, total_ref):
    basis = jnp.concatenate([left_ref[...], right_ref[...]], axis=1)
    product = jnp.dot(rows_ref[...], basis, preferred_element_type=jnp.float32)
    step = pl.program_id(0)

    @pl.when(step == 0)
    def _():
        total_ref[...] = product

    @pl.when(step > 0)
    def _():
        total_ref[...] += product

    @pl.when(step == pl.num_programs(0) - 1)
    def _():
        out_ref[...] = total_ref[...].astype(jnp.bfloat16)


def rotate(rows, left, right):
    count, long = rows.shape
    width = left.shape[1] + right.shape[1]
    depth = long // NY
    return pl.pallas_call(
        rotate_kernel,
        grid=(NY,),
        in_specs=[
            pl.BlockSpec((count, depth), lambda k: (0, k)),
            pl.BlockSpec((depth, left.shape[1]), lambda k: (k, 0)),
            pl.BlockSpec((depth, right.shape[1]), lambda k: (k, 0)),
        ],
        out_specs=pl.BlockSpec((count, width), lambda k: (0, 0)),
        out_shape=jax.ShapeDtypeStruct((count, width), jnp.bfloat16),
        scratch_shapes=[pltpu.VMEM((count, width), jnp.float32)],
        compiler_params=pltpu.CompilerParams(vmem_limit_bytes=VMEM),
        cost_estimate=pl.CostEstimate(
            flops=2 * count * long * width,
            bytes_accessed=2 * (count + width) * long,
            transcendentals=0,
        ),
    )(rows, left, right)


def on_device(activations, gradients, input_basis, output_basis):
    dp, mp = lax.axis_index("dp"), lax.axis_index("mp")
    core, x_lo, z, y = mp % 2, dp % 2, dp // 2 % NZ, dp // 2 // NZ
    step = 1 - 2 * core
    first = core == 0
    own = jnp.where(first, activations, gradients)
    same = send(jnp.where(x_lo == 0, input_basis, output_basis), DEAL_SAME)
    cross = send(jnp.where(x_lo == 0, output_basis, input_basis), DEAL_OTHER)
    share = jnp.concatenate([jnp.where(first, same, cross), jnp.where(first, cross, same)], axis=0)
    share, own = lax.optimization_barrier((share, own))
    other = send(own, RING_X)
    width = share.shape[1]
    half = width // 2
    short = [(share[:, half:],) * 2]
    short.append(hop(short[-1], RINGS_Z))
    left, short[-1] = lax.optimization_barrier((share[:, :half], short[-1]))
    for _ in range(NZ // 2 - 2):
        short.append(hop(short[-1], RINGS_Z))
    short.append((send(short[-1][0], RINGS_Z[0]), None))
    z_last = shift_gather(left, y, NY, SHIFTS_Y, 0)
    z_last, short[-1] = lax.optimization_barrier((z_last, short[-1]))
    long_z = [(z_last,) * 2]
    for _ in range(2):
        long_z.append(hop(long_z[-1], RINGS_Z))
    long_y = [(ring_blocks(short, z, step, NZ, 0),) * 2]
    long_y.append(hop(long_y[-1], RINGS_Y))
    long_z.append(hop(long_z[-1], RINGS_Z))
    long_y.append((send(long_y[-1][0], RINGS_Y[0]), None))
    long_z.append((send(long_z[-1][0], RINGS_Z[0]), None))
    z_last = ring_blocks(long_z, z, step, NZ, 1).reshape(-1, half)
    y_last = ring_blocks(long_y, y, step, NY, 0).reshape(-1, width - half)
    rotated_own, rotated_other = (rotate(rows, z_last, y_last) for rows in (own, other))
    mine, theirs = (rotated_own, rotated_other), (rotated_other, rotated_own)
    near = [send(half, SWAP) for half in mine]
    far = [send(half, PARTNER) for half in theirs]
    passed = [send(half, FORWARD) for half in far]
    z_blocks, y_blocks = coded_moments(
        core, (*mine, *near, *far, *passed), width // 3 // LANES * LANES
    )
    came_z = exchange(z_blocks, LINES_Z)
    came_y = shift(y_blocks, y, NY, SHIFTS_Y)
    left = shift(halfway([came_z], NY), y, NY, SHIFTS_Y)
    right = halfway(came_y, NZ)
    total = final(left, exchange(right, LINES_Z))
    return send(total, HOME)


def solution(mesh):
    in_specs = (P("dp", None), P("dp", None), P("dp", "mp"), P("dp", "mp"))
    out_specs = P("dp", "mp")
    return jax.shard_map(
        on_device, mesh=mesh, in_specs=in_specs, out_specs=out_specs, check_vma=False
    )
```
